32 devices in a mesh: blk: 8 (over z, y), tp: 4 (over x, core).
Axes of the slice: x: 2, y: 2, z: 4, core: 2. Of those that a mesh axis runs over, the one named last changes fastest.
Arguments:
- tokens: bfloat16 [3072, 4096], P('blk'), may hold values from -48 to 48
- w_query: bfloat16 [4096, 2048], P('blk', 'tp'), may hold values from -0.09375 to 0.09375
- key_weight: bfloat16 [4096, 512], P('blk', 'tp'), may hold values from -0.09375 to 0.09375
- value_weight: bfloat16 [4096, 512], P('blk', 'tp'), may hold values from -0.09375 to 0.09375
- w_output: bfloat16 [2048, 4096], P('tp', 'blk'), may hold values from -0.125 to 0.125
- out_grad: bfloat16 [3072, 4096], P('blk'), may hold values from -3 to 3
Outputs:
- attn_out: bfloat16 [3072, 4096], P('blk', 'tp')
- tokens_grad: bfloat16 [3072, 4096], P('blk', 'tp')
- query_grad: float32 [4096, 2048], P('blk', 'tp')
- key_grad: float32 [4096, 512], P('blk', 'tp')
- value_grad: float32 [4096, 512], P('blk', 'tp')
- output_grad: float32 [2048, 4096], P('tp', 'blk')
The draws below stay inside these ranges and needn't reach their ends.
All inputs are finite; a program needn't handle non-finite values.
Results may differ from the reference program's by a relative error of at most 0.005.
The reference program's roundings to bfloat16 on the way count: a program that leaves them out, or rounds other values in their place, can miss the bound.
Values may be sent and summed in bfloat16 or wider, within the bound.
A program may use at most 128 MiB of HBM per device.

```python
import math
import jax
import jax.numpy as jnp
from jax import lax

MODEL_WIDTH = 4096
HEAD_SIZE = 128
QUERY_HEADS = 16
KEY_VALUE_HEADS = 4
TOK = 384
TOKENS = 3072
N_BLK = 8


def draw_tokens(key, part):
    key = jax.random.fold_in(key, 11)
    base_key = jax.random.fold_in(key, 0)
    values = jax.random.normal(base_key, (TOKENS, MODEL_WIDTH), jnp.float32)
    values = jnp.clip(values, -6.0, 6.0)
    return values.astype(jnp.bfloat16)


def levels(rng, dims, cuts, least, top_value):
    gain = 1.0
    for axis_at, parts in cuts:
        heights = jax.random.uniform(jax.random.fold_in(jax.random.fold_in(rng, 6), axis_at), (parts,), jnp.float32, least / len(cuts), top_value / len(cuts))
        gain = gain * jnp.repeat(jnp.exp(heights), dims[axis_at] // parts).reshape((-1,) + (1,) * (len(dims) - 1 - axis_at))
    return gain


def centred(key, shape, scale, bound, cuts=(), held_as=jnp.bfloat16):
    gain = levels(key, shape, cuts, -0.22, 0.18) if cuts else 1.0
    values = jax.random.normal(key, shape, jnp.float32) * scale * gain
    return jnp.minimum(jnp.maximum(values, -bound), bound).astype(held_as)


def setup_inputs(seed: int = 0) -> dict:
    arg_keys = jax.random.split(jax.random.key(seed), 7)
    tokens = draw_tokens(jax.random.fold_in(arg_keys[6], 71), 0)
    w_query = centred(arg_keys[1], (MODEL_WIDTH, QUERY_HEADS * HEAD_SIZE), MODEL_WIDTH ** -0.5, 0.09375, ((0, 8), (1, 4)))
    key_weight = centred(arg_keys[2], (MODEL_WIDTH, KEY_VALUE_HEADS * HEAD_SIZE), MODEL_WIDTH ** -0.5, 0.09375, ((0, 8), (1, 4)))
    value_weight = centred(arg_keys[3], (MODEL_WIDTH, KEY_VALUE_HEADS * HEAD_SIZE), MODEL_WIDTH ** -0.5, 0.09375, ((0, 8), (1, 4)))
    w_output = centred(arg_keys[4], (QUERY_HEADS * HEAD_SIZE, MODEL_WIDTH), (QUERY_HEADS * HEAD_SIZE) ** -0.5, 0.125, ((0, 4), (1, 8)))
    out_grad = centred(arg_keys[5], (TOKENS, MODEL_WIDTH), 0.5, 3.0, ((0, 8),))
    return dict(tokens=tokens, w_query=w_query, key_weight=key_weight, value_weight=value_weight, w_output=w_output, out_grad=out_grad)


def rounded(value):
    return lax.optimization_barrier(value.astype(jnp.bfloat16))

def micro_batch(tokens, out_grad, w_query, key_weight, value_weight, w_output):
    sequence_length = tokens.shape[0]
    group_width = QUERY_HEADS // KEY_VALUE_HEADS
    score_scale = 1.0 / math.sqrt(HEAD_SIZE)
    query_activation = rounded(jnp.dot(tokens, w_query, preferred_element_type=jnp.float32))
    key_activation = rounded(jnp.dot(tokens, key_weight, preferred_element_type=jnp.float32))
    value_activation = rounded(jnp.dot(tokens, value_weight, preferred_element_type=jnp.float32))
    query_head_rows = query_activation.astype(jnp.float32).reshape(sequence_length, KEY_VALUE_HEADS, group_width, HEAD_SIZE)
    key_head_rows = key_activation.astype(jnp.float32).reshape(sequence_length, KEY_VALUE_HEADS, HEAD_SIZE)
    value_head_rows = value_activation.astype(jnp.float32).reshape(sequence_length, KEY_VALUE_HEADS, HEAD_SIZE)
    scores = jnp.einsum('tkgd,skd->kgts', query_head_rows, key_head_rows) * score_scale
    row_index = lax.broadcasted_iota(jnp.int32, scores.shape, 2)
    col_index = lax.broadcasted_iota(jnp.int32, scores.shape, 3)
    scores = jnp.where(col_index <= row_index, scores, -jnp.inf)
    row_max = lax.optimization_barrier(jnp.max(scores, axis=-1, keepdims=True))
    powered = jnp.exp(scores - row_max)
    probs = powered / lax.optimization_barrier(jnp.sum(powered, axis=-1, keepdims=True))
    probs_b = rounded(probs)
    probabilities_wide = probs_b.astype(jnp.float32)
    head_mix = rounded(jnp.einsum('kgts,skd->tkgd', probabilities_wide, value_head_rows)).reshape(sequence_length, QUERY_HEADS * HEAD_SIZE)
    attn_out = jnp.dot(head_mix, w_output, preferred_element_type=jnp.float32).astype(jnp.bfloat16)
    mixture_gradient = rounded(jnp.dot(out_grad, w_output.T, preferred_element_type=jnp.float32))
    heads_gradient = mixture_gradient.astype(jnp.float32).reshape(sequence_length, KEY_VALUE_HEADS, group_width, HEAD_SIZE)
    grad_probs = jnp.einsum('tkgd,skd->kgts', heads_gradient, value_head_rows)
    row_delta = lax.optimization_barrier(jnp.sum(probs * grad_probs, axis=-1, keepdims=True))
    scores_gradient = rounded(probs * (grad_probs - row_delta) * score_scale).astype(jnp.float32)
    grad_query = jnp.einsum('kgts,skd->tkgd', scores_gradient, key_head_rows).astype(jnp.bfloat16).reshape(sequence_length, QUERY_HEADS * HEAD_SIZE)
    key_gradient = jnp.einsum('uxyi,yuxz->iuz', scores_gradient, query_head_rows).astype(jnp.bfloat16).reshape(sequence_length, KEY_VALUE_HEADS * HEAD_SIZE)
    value_gradient = jnp.einsum('uxyi,yuxz->iuz', probabilities_wide, heads_gradient).astype(jnp.bfloat16).reshape(sequence_length, KEY_VALUE_HEADS * HEAD_SIZE)
    tokens_grad = (jnp.dot(grad_query, w_query.T, preferred_element_type=jnp.float32) + jnp.dot(key_gradient, key_weight.T, preferred_element_type=jnp.float32) + jnp.dot(value_gradient, value_weight.T, preferred_element_type=jnp.float32)).astype(jnp.bfloat16)
    grads = (jnp.dot(tokens.T, grad_query, preferred_element_type=jnp.float32), jnp.dot(tokens.T, key_gradient, preferred_element_type=jnp.float32), jnp.dot(tokens.T, value_gradient, preferred_element_type=jnp.float32), jnp.dot(head_mix.T, out_grad, preferred_element_type=jnp.float32))
    return ((attn_out, tokens_grad), grads)

def reference(tokens, w_query, key_weight, value_weight, w_output, out_grad):
    token_blocks = tokens.reshape(N_BLK, TOK, MODEL_WIDTH)
    grad_blocks = out_grad.reshape(N_BLK, TOK, MODEL_WIDTH)

    def one_batch(carry_sums, inputs_pair):
        outputs, grads = micro_batch(inputs_pair[0], inputs_pair[1], w_query, key_weight, value_weight, w_output)
        return (tuple((total + grad for total, grad in zip(carry_sums, grads))), outputs)
    initial_sums = (jnp.zeros((MODEL_WIDTH, QUERY_HEADS * HEAD_SIZE), jnp.float32), jnp.zeros((MODEL_WIDTH, KEY_VALUE_HEADS * HEAD_SIZE), jnp.float32), jnp.zeros((MODEL_WIDTH, KEY_VALUE_HEADS * HEAD_SIZE), jnp.float32), jnp.zeros((QUERY_HEADS * HEAD_SIZE, MODEL_WIDTH), jnp.float32))
    final_sums, outputs = lax.scan(one_batch, initial_sums, (token_blocks, grad_blocks))
    attn_out = outputs[0].reshape(TOKENS, MODEL_WIDTH)
    tokens_grad = outputs[1].reshape(TOKENS, MODEL_WIDTH)
    return (attn_out, tokens_grad, final_sums[0], final_sums[1], final_sums[2], final_sums[3])
```

```python
import math

import jax
import jax.numpy as jnp
from jax import lax
from jax.sharding import PartitionSpec as P

HEAD_SIZE = 128


def transposed_product(first_operand, second_operand):
    return lax.dot_general(
        first_operand, second_operand, (((1,), (1,)), ((), ())), preferred_element_type=jnp.float32
    )


def leading_product(first_operand, second_operand):
    return lax.dot_general(
        first_operand, second_operand, (((0,), (0,)), ((), ())), preferred_element_type=jnp.float32
    )


def causal_probs(query_block, key_head_rows, first_row, score_scale):
    scores = (
        jnp.einsum("tkgd,skd->kgts", query_block, key_head_rows, preferred_element_type=jnp.float32)
        * score_scale
    )
    row_index = first_row + lax.broadcasted_iota(jnp.int32, scores.shape, 2)
    col_index = lax.broadcasted_iota(jnp.int32, scores.shape, 3)
    scores = jnp.where(col_index <= row_index, scores, -jnp.inf)
    row_max = jnp.max(scores, axis=-1, keepdims=True)
    powered = jnp.exp(scores - row_max)
    return powered / jnp.sum(powered, axis=-1, keepdims=True)


def column_blocks(tokens, out_grad, tp_count, blk_count):
    rows, width = tokens.shape
    part = rows // tp_count
    cols = width // blk_count
    first = lax.axis_index("tp") * part
    sent = jnp.stack(
        [
            lax.dynamic_slice_in_dim(tokens, first, part, 0),
            lax.dynamic_slice_in_dim(out_grad, first, part, 0),
        ]
    )
    sent = sent.reshape(2, part, blk_count, cols).transpose(2, 0, 1, 3)
    landed = lax.all_to_all(sent, "blk", 0, 0, tiled=True)
    whole = lax.all_gather(landed, "tp", axis=0)
    whole = jnp.transpose(whole, (2, 1, 0, 3, 4)).reshape(2, blk_count * rows, cols)
    return (whole[0], whole[1])


def on_device(tokens, w_query, key_weight, value_weight, w_output, out_grad):
    sequence_length = tokens.shape[0]
    head_cols = w_query.shape[1]
    kv_cols = key_weight.shape[1]
    local_kv = kv_cols // HEAD_SIZE
    group_width = head_cols // kv_cols
    block_count = sequence_length // sequence_length
    score_scale = 1.0 / math.sqrt(HEAD_SIZE)
    tp_count = lax.axis_size("tp")
    blk_count = lax.axis_size("blk")
    weight_block = jnp.concatenate([w_query, key_weight, value_weight, w_output.T], axis=1)
    weight_rows = lax.all_gather(weight_block, "blk", axis=0, tiled=True)
    query_rows = weight_rows[:, :head_cols]
    key_rows = weight_rows[:, head_cols : head_cols + kv_cols]
    value_rows = weight_rows[:, head_cols + kv_cols : head_cols + 2 * kv_cols]
    output_cols = weight_rows[:, head_cols + 2 * kv_cols :]
    inputs_by_cols = column_blocks(tokens, out_grad, tp_count, blk_count)
    query_full = jnp.dot(tokens, query_rows, preferred_element_type=jnp.float32)
    key_full = jnp.dot(tokens, key_rows, preferred_element_type=jnp.float32)
    value_full = jnp.dot(tokens, value_rows, preferred_element_type=jnp.float32)
    query_activation = query_full.astype(jnp.bfloat16)
    query_head_rows = query_activation.reshape(sequence_length, local_kv, group_width, HEAD_SIZE)
    key_activation = key_full.astype(jnp.bfloat16)
    key_head_rows = key_activation.reshape(sequence_length, local_kv, HEAD_SIZE)
    value_head_rows = value_full.astype(jnp.bfloat16).reshape(sequence_length, local_kv, HEAD_SIZE)
    block_ids = jnp.arange(block_count, dtype=jnp.int32)

    def forward_block(ignored, block_index):
        first_row = block_index * sequence_length
        soft_weights = causal_probs(query_head_rows, key_head_rows, first_row, score_scale).astype(
            jnp.bfloat16
        )
        head_block = jnp.einsum(
            "kgts,skd->tkgd", soft_weights, value_head_rows, preferred_element_type=jnp.float32
        )
        return (ignored, head_block.astype(jnp.bfloat16))

    ignored_carry, mix_blocks = lax.scan(forward_block, jnp.zeros((), jnp.int32), block_ids)
    head_mix = mix_blocks.reshape(sequence_length, head_cols)
    out_term = transposed_product(head_mix, output_cols)
    attn_out = lax.psum_scatter(out_term, "tp", scatter_dimension=1, tiled=True).astype(
        jnp.bfloat16
    )
    heads_gradient = (
        jnp.dot(out_grad, output_cols, preferred_element_type=jnp.float32)
        .astype(jnp.bfloat16)
        .reshape(sequence_length, local_kv, group_width, HEAD_SIZE)
    )

    def backward_block(kv_sums, block_index):
        first_row = block_index * sequence_length
        probs = causal_probs(query_head_rows, key_head_rows, first_row, score_scale)
        soft_weights = probs.astype(jnp.bfloat16)
        grad_probs = jnp.einsum(
            "tkgd,skd->kgts", heads_gradient, value_head_rows, preferred_element_type=jnp.float32
        )
        row_delta = jnp.sum(probs * grad_probs, axis=-1, keepdims=True)
        scores_gradient = (probs * (grad_probs - row_delta) * score_scale).astype(jnp.bfloat16)
        grad_query = jnp.einsum(
            "kgts,skd->tkgd", scores_gradient, key_head_rows, preferred_element_type=jnp.float32
        )
        key_total = kv_sums[0] + jnp.einsum(
            "uxyi,yuxz->iuz", scores_gradient, query_head_rows, preferred_element_type=jnp.float32
        )
        value_total = kv_sums[1] + jnp.einsum(
            "uxyi,yuxz->iuz", soft_weights, heads_gradient, preferred_element_type=jnp.float32
        )
        return ((key_total, value_total), grad_query.astype(jnp.bfloat16))

    empty_kv = jnp.zeros((sequence_length, local_kv, HEAD_SIZE), jnp.float32)
    kv_totals, query_blocks = lax.scan(backward_block, (empty_kv, empty_kv), block_ids)
    grad_query = query_blocks.reshape(sequence_length, head_cols)
    key_gradient = kv_totals[0].astype(jnp.bfloat16).reshape(sequence_length, kv_cols)
    value_gradient = kv_totals[1].astype(jnp.bfloat16).reshape(sequence_length, kv_cols)
    input_term = (
        transposed_product(grad_query, query_rows)
        + transposed_product(key_gradient, key_rows)
        + transposed_product(value_gradient, value_rows)
    )
    tokens_grad = lax.psum_scatter(input_term, "tp", scatter_dimension=1, tiled=True).astype(
        jnp.bfloat16
    )
    mix_all = lax.all_gather(head_mix, "blk", axis=0, tiled=True)
    joined_grads = jnp.concatenate([grad_query, key_gradient, value_gradient], axis=1)
    grads_all = lax.all_gather(joined_grads, "blk", axis=0, tiled=True)
    tokens_cols, out_grad_cols = inputs_by_cols
    joint_grad = leading_product(tokens_cols, grads_all)
    query_grad = joint_grad[:, :head_cols]
    key_grad = joint_grad[:, head_cols : head_cols + kv_cols]
    value_grad = joint_grad[:, head_cols + kv_cols :]
    output_grad = leading_product(mix_all, out_grad_cols)
    return (attn_out, tokens_grad, query_grad, key_grad, value_grad, output_grad)


def solution(mesh):
    placed = (
        P("blk", None),
        P("blk", "tp"),
        P("blk", "tp"),
        P("blk", "tp"),
        P("tp", "blk"),
        P("blk", None),
    )
    return jax.shard_map(
        on_device,
        mesh=mesh,
        in_specs=placed,
        out_specs=(
            P("blk", "tp"),
            P("blk", "tp"),
            P("blk", "tp"),
            P("blk", "tp"),
            P("blk", "tp"),
            P("tp", "blk"),
        ),
        check_vma=False,
    )
```

```python
import functools
import math

import jax
import jax.numpy as jnp
from jax import lax
from jax.experimental import pallas as pl
from jax.experimental.pallas import tpu as pltpu
from jax.sharding import PartitionSpec as P

HEAD_SIZE = 128


def transposed_product(first_operand, second_operand):
    return lax.dot_general(
        first_operand, second_operand, (((1,), (1,)), ((), ())), preferred_element_type=jnp.float32
    )


def leading_product(first_operand, second_operand):
    return lax.dot_general(
        first_operand, second_operand, (((0,), (0,)), ((), ())), preferred_element_type=jnp.float32
    )


def causal_probs(query_block, key_head_rows, first_row, score_scale):
    scores = (
        jnp.einsum("tkgd,skd->kgts", query_block, key_head_rows, preferred_element_type=jnp.float32)
        * score_scale
    )
    row_index = first_row + lax.broadcasted_iota(jnp.int32, scores.shape, 2)
    col_index = lax.broadcasted_iota(jnp.int32, scores.shape, 3)
    scores = jnp.where(col_index <= row_index, scores, -jnp.inf)
    row_max = jnp.max(scores, axis=-1, keepdims=True)
    powered = jnp.exp(scores - row_max)
    return powered / jnp.sum(powered, axis=-1, keepdims=True)


def remote(src, dst, send, recv, dest):
    return pltpu.make_async_remote_copy(
        src_ref=src,
        dst_ref=dst,
        send_sem=send,
        recv_sem=recv,
        device_id={"blk": dest},
        device_id_type=pl.DeviceIdType.MESH,
    )


def greet(n):
    me = lax.axis_index("blk")
    barrier = pltpu.get_barrier_semaphore()
    for offset in range(1, n):
        pl.semaphore_signal(
            barrier,
            inc=1,
            device_id={"blk": lax.rem(me + offset, n)},
            device_id_type=pl.DeviceIdType.MESH,
        )
    pl.semaphore_wait(barrier, n - 1)


def chain_gather(n, own, out, chain_send, chain_recv, side_send, side_recv, own_sem):
    me = lax.axis_index("blk")
    length = n // 2
    place, side = me // 2, lax.rem(me, 2)
    other = place * 2 + (1 - side)

    def along(way, origin, first):
        src = own if first else out.at[origin * 2 + side]
        step = 2 if way == 0 else -2
        return remote(
            src, out.at[origin * 2 + side], chain_send.at[way, origin], chain_recv.at[origin], me + step
        )

    def across(origin, first):
        src = own if first else out.at[origin * 2 + side]
        return remote(
            src, out.at[origin * 2 + side], side_send.at[origin], side_recv.at[origin], other
        )

    can = (place + 1 < length, place >= 1)
    for way in range(2):
        @pl.when(can[way])
        def _():
            along(way, place, True).start()

    across(place, True).start()
    mine = pltpu.make_async_copy(own, out.at[me], own_sem)
    mine.start()
    for step in range(1, length):
        for way in range(2):
            origin = place - step if way == 0 else place + step
            there = origin >= 0 if way == 0 else origin < length

            @pl.when(there)
            def _():
                along(way, origin, False).wait_recv()

            @pl.when(jnp.logical_and(there, can[way]))
            def _():
                along(way, origin, False).start()

            @pl.when(there)
            def _():
                across(origin, False).start()

    def finish():
        mine.wait()
        for step in range(length):
            for way in range(2):
                if step == 0 and way == 1:
                    continue
                origin = place - step if way == 0 else place + step
                there = origin >= 0 if way == 0 else origin < length

                @pl.when(there)
                def _():
                    across(origin, step == 0).wait_send()

            for way in range(2):
                origin = place - step if way == 0 else place + step
                there = origin >= 0 if way == 0 else origin < length

                @pl.when(jnp.logical_and(there, can[way]))
                def _():
                    along(way, origin, step == 0).wait_send()

        for origin in range(length):
            landed = out.at[origin * 2 + (1 - side)]
            remote(landed, landed, side_send.at[origin], side_recv.at[origin], other).wait_recv()

    return finish


def gather_semaphores(n):
    length = n // 2
    return [
        pltpu.SemaphoreType.DMA((2, length)),
        pltpu.SemaphoreType.DMA((length,)),
        pltpu.SemaphoreType.DMA((length,)),
        pltpu.SemaphoreType.DMA((length,)),
        pltpu.SemaphoreType.DMA,
    ]


def first_kernel(n, parts, weights, tokens, out_grad, out, landed, *sems):
    gather_sems, (part_send, part_recv, part_own) = sems[:5], sems[5:]
    me = lax.axis_index("blk")
    rows = tokens.shape[0] // parts
    cols = tokens.shape[1] // n
    first = pl.multiple_of(lax.axis_index("tp") * rows, rows)
    greet(n)

    def part(which, dest):
        at = pl.multiple_of(dest * cols, cols)
        return (tokens, out_grad)[which].at[pl.ds(first, rows), pl.ds(at, cols)]

    def sending(which, offset):
        dest = lax.rem(me + offset, n)
        return remote(
            part(which, dest),
            landed.at[which, me],
            part_send.at[which, offset],
            part_recv.at[which, offset],
            dest,
        )

    own_parts = [
        pltpu.make_async_copy(part(which, me), landed.at[which, me], part_own.at[which])
        for which in range(2)
    ]
    for copy in own_parts:
        copy.start()
    for which in range(2):
        for offset in range(1, n):
            sending(which, offset).start()
    finish = chain_gather(n, weights, out, *gather_sems)
    finish()
    for copy in own_parts:
        copy.wait()
    for which in range(2):
        for offset in range(1, n):
            sending(which, offset).wait_send()
            origin = lax.rem(me + n - offset, n)
            here = landed.at[which, origin]
            remote(
                here, here, part_send.at[which, offset], part_recv.at[which, offset], origin
            ).wait_recv()


def second_kernel(n, own, out, *sems):
    greet(n)
    chain_gather(n, own, out, *sems)()


def gather_inputs(weights, tokens, out_grad, tp_count, n):
    rows = tokens.shape[0] // tp_count
    cols = tokens.shape[1] // n
    anywhere = pl.BlockSpec(memory_space=pl.ANY)
    gathered, landed = pl.pallas_call(
        functools.partial(first_kernel, n, tp_count),
        out_shape=(
            jax.ShapeDtypeStruct((n,) + weights.shape, weights.dtype),
            jax.ShapeDtypeStruct((2, n, rows, cols), tokens.dtype),
        ),
        in_specs=[anywhere] * 3,
        out_specs=(anywhere, anywhere),
        scratch_shapes=gather_semaphores(n)
        + [
            pltpu.SemaphoreType.DMA((2, n)),
            pltpu.SemaphoreType.DMA((2, n)),
            pltpu.SemaphoreType.DMA((2,)),
        ],
        compiler_params=pltpu.CompilerParams(collective_id=0, has_side_effects=True),
        cost_estimate=pl.CostEstimate(flops=0, bytes_accessed=300_000_000, transcendentals=0),
        name="gather_inputs",
    )(weights, tokens, out_grad)
    return gathered.reshape(n * weights.shape[0], weights.shape[1]), landed


def gather_grads(own, n):
    anywhere = pl.BlockSpec(memory_space=pl.ANY)
    gathered = pl.pallas_call(
        functools.partial(second_kernel, n),
        out_shape=jax.ShapeDtypeStruct((n,) + own.shape, own.dtype),
        in_specs=[anywhere],
        out_specs=anywhere,
        scratch_shapes=gather_semaphores(n),
        compiler_params=pltpu.CompilerParams(collective_id=1, has_side_effects=True),
        cost_estimate=pl.CostEstimate(flops=0, bytes_accessed=250_000_000, transcendentals=0),
        name="gather_grads",
    )(own)
    return gathered.reshape(n * own.shape[0], own.shape[1])


def on_device(tokens, w_query, key_weight, value_weight, w_output, out_grad):
    sequence_length = tokens.shape[0]
    head_cols = w_query.shape[1]
    kv_cols = key_weight.shape[1]
    local_kv = kv_cols // HEAD_SIZE
    group_width = head_cols // kv_cols
    block_count = sequence_length // sequence_length
    score_scale = 1.0 / math.sqrt(HEAD_SIZE)
    tp_count = lax.axis_size("tp")
    blk_count = lax.axis_size("blk")
    weight_block = jnp.concatenate([w_query, key_weight, value_weight, w_output.T], axis=1)
    weight_rows, landed = gather_inputs(weight_block, tokens, out_grad, tp_count, blk_count)
    joint_cols = head_cols + 2 * kv_cols
    joint_rows = weight_rows[:, :joint_cols]
    output_cols = weight_rows[:, joint_cols:]
    block_cols = landed.shape[3]
    inputs_by_cols = lax.all_gather(landed, "tp", axis=0)
    inputs_by_cols = jnp.transpose(inputs_by_cols, (1, 2, 0, 3, 4)).reshape(
        2, blk_count * sequence_length, block_cols
    )
    joint_full = jnp.dot(tokens, joint_rows, preferred_element_type=jnp.float32)
    query_full = joint_full[:, :head_cols]
    key_full = joint_full[:, head_cols : head_cols + kv_cols]
    value_full = joint_full[:, head_cols + kv_cols :]
    query_activation = query_full.astype(jnp.bfloat16)
    query_head_rows = query_activation.reshape(sequence_length, local_kv, group_width, HEAD_SIZE)
    key_activation = key_full.astype(jnp.bfloat16)
    key_head_rows = key_activation.reshape(sequence_length, local_kv, HEAD_SIZE)
    value_head_rows = value_full.astype(jnp.bfloat16).reshape(sequence_length, local_kv, HEAD_SIZE)
    block_ids = jnp.arange(block_count, dtype=jnp.int32)

    def forward_block(ignored, block_index):
        first_row = block_index * sequence_length
        soft_weights = causal_probs(query_head_rows, key_head_rows, first_row, score_scale).astype(
            jnp.bfloat16
        )
        head_block = jnp.einsum(
            "kgts,skd->tkgd", soft_weights, value_head_rows, preferred_element_type=jnp.float32
        )
        return (ignored, head_block.astype(jnp.bfloat16))

    ignored_carry, mix_blocks = lax.scan(forward_block, jnp.zeros((), jnp.int32), block_ids)
    head_mix = mix_blocks.reshape(sequence_length, head_cols)
    out_term = transposed_product(head_mix, output_cols)
    attn_out = lax.psum_scatter(out_term, "tp", scatter_dimension=1, tiled=True).astype(
        jnp.bfloat16
    )
    heads_gradient = (
        jnp.dot(out_grad, output_cols, preferred_element_type=jnp.float32)
        .astype(jnp.bfloat16)
        .reshape(sequence_length, local_kv, group_width, HEAD_SIZE)
    )

    def backward_block(kv_sums, block_index):
        first_row = block_index * sequence_length
        probs = causal_probs(query_head_rows, key_head_rows, first_row, score_scale)
        soft_weights = probs.astype(jnp.bfloat16)
        grad_probs = jnp.einsum(
            "tkgd,skd->kgts", heads_gradient, value_head_rows, preferred_element_type=jnp.float32
        )
        row_delta = jnp.sum(probs * grad_probs, axis=-1, keepdims=True)
        scores_gradient = (probs * (grad_probs - row_delta) * score_scale).astype(jnp.bfloat16)
        grad_query = jnp.einsum(
            "kgts,skd->tkgd", scores_gradient, key_head_rows, preferred_element_type=jnp.float32
        )
        key_total = kv_sums[0] + jnp.einsum(
            "uxyi,yuxz->iuz", scores_gradient, query_head_rows, preferred_element_type=jnp.float32
        )
        value_total = kv_sums[1] + jnp.einsum(
            "uxyi,yuxz->iuz", soft_weights, heads_gradient, preferred_element_type=jnp.float32
        )
        return ((key_total, value_total), grad_query.astype(jnp.bfloat16))

    empty_kv = jnp.zeros((sequence_length, local_kv, HEAD_SIZE), jnp.float32)
    kv_totals, query_blocks = lax.scan(backward_block, (empty_kv, empty_kv), block_ids)
    grad_query = query_blocks.reshape(sequence_length, head_cols)
    key_gradient = kv_totals[0].astype(jnp.bfloat16).reshape(sequence_length, kv_cols)
    value_gradient = kv_totals[1].astype(jnp.bfloat16).reshape(sequence_length, kv_cols)
    joined_grads = jnp.concatenate([grad_query, key_gradient, value_gradient], axis=1)
    input_term = transposed_product(joined_grads, joint_rows)
    tokens_grad = lax.psum_scatter(input_term, "tp", scatter_dimension=1, tiled=True).astype(
        jnp.bfloat16
    )
    grads_all = gather_grads(jnp.concatenate([joined_grads, head_mix], axis=1), blk_count)
    tokens_cols, out_grad_cols = inputs_by_cols[0], inputs_by_cols[1]
    joint_grad = leading_product(tokens_cols, grads_all[:, :joint_cols])
    query_grad = joint_grad[:, :head_cols]
    key_grad = joint_grad[:, head_cols : head_cols + kv_cols]
    value_grad = joint_grad[:, head_cols + kv_cols :]
    output_grad = leading_product(grads_all[:, joint_cols:], out_grad_cols)
    return (attn_out, tokens_grad, query_grad, key_grad, value_grad, output_grad)


def solution(mesh):
    placed = (
        P("blk", None),
        P("blk", "tp"),
        P("blk", "tp"),
        P("blk", "tp"),
        P("tp", "blk"),
        P("blk", None),
    )
    return jax.shard_map(
        on_device,
        mesh=mesh,
        in_specs=placed,
        out_specs=(
            P("blk", "tp"),
            P("blk", "tp"),
            P("blk", "tp"),
            P("blk", "tp"),
            P("blk", "tp"),
            P("tp", "blk"),
        ),
        check_vma=False,
    )
```

```python
import functools
import math

import jax
import jax.numpy as jnp
from jax import lax
from jax.experimental import pallas as pl
from jax.experimental.pallas import tpu as pltpu
from jax.sharding import PartitionSpec as P

HEAD_SIZE = 128


def transposed_product(first_operand, second_operand):
    return lax.dot_general(
        first_operand, second_operand, (((1,), (1,)), ((), ())), preferred_element_type=jnp.float32
    )


def leading_product(first_operand, second_operand):
    return lax.dot_general(
        first_operand, second_operand, (((0,), (0,)), ((), ())), preferred_element_type=jnp.float32
    )


def causal_probs(query_block, key_head_rows, first_row, score_scale):
    scores = (
        jnp.einsum("tkgd,skd->kgts", query_block, key_head_rows, preferred_element_type=jnp.float32)
        * score_scale
    )
    row_index = first_row + lax.broadcasted_iota(jnp.int32, scores.shape, 2)
    col_index = lax.broadcasted_iota(jnp.int32, scores.shape, 3)
    scores = jnp.where(col_index <= row_index, scores, -jnp.inf)
    row_max = jnp.max(scores, axis=-1, keepdims=True)
    powered = jnp.exp(scores - row_max)
    return powered / jnp.sum(powered, axis=-1, keepdims=True)


def remote(src, dst, send, recv, dest, axis="blk"):
    return pltpu.make_async_remote_copy(
        src_ref=src,
        dst_ref=dst,
        send_sem=send,
        recv_sem=recv,
        device_id={axis: dest},
        device_id_type=pl.DeviceIdType.MESH,
    )


def greet(n, parts=1):
    me = lax.axis_index("blk")
    barrier = pltpu.get_barrier_semaphore()
    for offset in range(1, n):
        pl.semaphore_signal(
            barrier,
            inc=1,
            device_id={"blk": lax.rem(me + offset, n)},
            device_id_type=pl.DeviceIdType.MESH,
        )
    mate = lax.axis_index("tp")
    for offset in range(1, parts):
        pl.semaphore_signal(
            barrier,
            inc=1,
            device_id={"tp": lax.rem(mate + offset, parts)},
            device_id_type=pl.DeviceIdType.MESH,
        )
    pl.semaphore_wait(barrier, n - 1 + parts - 1)


def chain_gather(n, own, out, chain_send, chain_recv, side_send, side_recv, own_sem, begin=None, between=None):
    me = lax.axis_index("blk")
    length = n // 2
    place, side = me // 2, lax.rem(me, 2)
    other = place * 2 + (1 - side)

    def along(way, origin, first):
        src = own if first else out.at[origin * 2 + side]
        step = 2 if way == 0 else -2
        return remote(
            src, out.at[origin * 2 + side], chain_send.at[way, origin], chain_recv.at[origin], me + step
        )

    def across(origin, first):
        src = own if first else out.at[origin * 2 + side]
        return remote(
            src, out.at[origin * 2 + side], side_send.at[origin], side_recv.at[origin], other
        )

    can = (place + 1 < length, place >= 1)
    for way in range(2):
        @pl.when(can[way])
        def _():
            along(way, place, True).start()

    if begin is not None:
        begin()
    across(place, True).start()
    mine = pltpu.make_async_copy(own, out.at[me], own_sem)
    mine.start()
    for step in range(1, length):
        for way in range(2):
            origin = place - step if way == 0 else place + step
            there = origin >= 0 if way == 0 else origin < length

            @pl.when(there)
            def _():
                along(way, origin, False).wait_recv()

            @pl.when(jnp.logical_and(there, can[way]))
            def _():
                along(way, origin, False).start()

            @pl.when(there)
            def _():
                across(origin, False).start()

        if between is not None:
            between(step)

    def finish():
        mine.wait()
        for step in range(length):
            for way in range(2):
                if step == 0 and way == 1:
                    continue
                origin = place - step if way == 0 else place + step
                there = origin >= 0 if way == 0 else origin < length

                @pl.when(there)
                def _():
                    across(origin, step == 0).wait_send()

            for way in range(2):
                origin = place - step if way == 0 else place + step
                there = origin >= 0 if way == 0 else origin < length

                @pl.when(jnp.logical_and(there, can[way]))
                def _():
                    along(way, origin, step == 0).wait_send()

        for origin in range(length):
            landed = out.at[origin * 2 + (1 - side)]
            remote(landed, landed, side_send.at[origin], side_recv.at[origin], other).wait_recv()

    return finish


def gather_semaphores(n):
    length = n // 2
    return [
        pltpu.SemaphoreType.DMA((2, length)),
        pltpu.SemaphoreType.DMA((length,)),
        pltpu.SemaphoreType.DMA((length,)),
        pltpu.SemaphoreType.DMA((length,)),
        pltpu.SemaphoreType.DMA,
    ]


def first_kernel(n, parts, weights, tokens, out_grad, out, landed, *sems):
    gather_sems, (part_send, part_recv, part_own, mate_send, mate_recv) = sems[:5], sems[5:]
    me = lax.axis_index("blk")
    mate = lax.axis_index("tp")
    rows = tokens.shape[0] // parts
    cols = tokens.shape[1] // n
    first = pl.multiple_of(mate * rows, rows)
    greet(n, parts)

    def part(which, dest):
        at = pl.multiple_of(dest * cols, cols)
        return (tokens, out_grad)[which].at[pl.ds(first, rows), pl.ds(at, cols)]

    def sending(which, offset):
        dest = lax.rem(me + offset, n)
        return remote(
            part(which, dest),
            landed.at[which, me, mate],
            part_send.at[which, offset],
            part_recv.at[which, offset],
            dest,
        )

    def arriving(which, offset):
        origin = lax.rem(me + n - offset, n)
        here = landed.at[which, origin, mate]
        return remote(here, here, part_send.at[which, offset], part_recv.at[which, offset], origin)

    def sharing(offset, other):
        here = landed.at[:, lax.rem(me + n - offset, n), mate]
        dest = lax.rem(mate + other, parts)
        return remote(here, here, mate_send.at[offset, other], mate_recv.at[offset, other], dest, "tp")

    def shared(offset, other):
        source = lax.rem(mate + parts - other, parts)
        here = landed.at[:, lax.rem(me + n - offset, n), source]
        return remote(here, here, mate_send.at[offset, other], mate_recv.at[offset, other], source, "tp")

    own_parts = [
        pltpu.make_async_copy(part(which, me), landed.at[which, me, mate], part_own.at[which])
        for which in range(2)
    ]
    steps = n // 2 - 1
    share = -(-(n - 1) // max(steps, 1))

    def begin():
        for copy in own_parts:
            copy.start()
        for offset in range(1, n):
            for which in range(2):
                sending(which, offset).start()
        for copy in own_parts:
            copy.wait()
        for other in range(1, parts):
            sharing(0, other).start()

    def pass_on(offsets):
        for offset in offsets:
            for which in range(2):
                arriving(which, offset).wait_recv()
            for other in range(1, parts):
                sharing(offset, other).start()

    def between(step):
        pass_on(range(1 + (step - 1) * share, min(1 + step * share, n)))

    finish = chain_gather(n, weights, out, *gather_sems, begin=begin, between=between)
    if steps == 0:
        pass_on(range(1, n))
    finish()
    for offset in range(1, n):
        for which in range(2):
            sending(which, offset).wait_send()
    for offset in range(n):
        for other in range(1, parts):
            sharing(offset, other).wait_send()
            shared(offset, other).wait_recv()


def second_kernel(n, own, out, *sems):
    greet(n)
    chain_gather(n, own, out, *sems)()


def gather_inputs(weights, tokens, out_grad, tp_count, n):
    rows = tokens.shape[0] // tp_count
    cols = tokens.shape[1] // n
    anywhere = pl.BlockSpec(memory_space=pl.ANY)
    gathered, landed = pl.pallas_call(
        functools.partial(first_kernel, n, tp_count),
        out_shape=(
            jax.ShapeDtypeStruct((n,) + weights.shape, weights.dtype),
            jax.ShapeDtypeStruct((2, n, tp_count, rows, cols), tokens.dtype),
        ),
        in_specs=[anywhere] * 3,
        out_specs=(anywhere, anywhere),
        scratch_shapes=gather_semaphores(n)
        + [
            pltpu.SemaphoreType.DMA((2, n)),
            pltpu.SemaphoreType.DMA((2, n)),
            pltpu.SemaphoreType.DMA((2,)),
            pltpu.SemaphoreType.DMA((n, tp_count)),
            pltpu.SemaphoreType.DMA((n, tp_count)),
        ],
        compiler_params=pltpu.CompilerParams(collective_id=0, has_side_effects=True),
        cost_estimate=pl.CostEstimate(flops=0, bytes_accessed=300_000_000, transcendentals=0),
        name="gather_inputs",
    )(weights, tokens, out_grad)
    return gathered.reshape(n * weights.shape[0], weights.shape[1]), landed


def gather_grads(own, n):
    anywhere = pl.BlockSpec(memory_space=pl.ANY)
    gathered = pl.pallas_call(
        functools.partial(second_kernel, n),
        out_shape=jax.ShapeDtypeStruct((n,) + own.shape, own.dtype),
        in_specs=[anywhere],
        out_specs=anywhere,
        scratch_shapes=gather_semaphores(n),
        compiler_params=pltpu.CompilerParams(collective_id=1, has_side_effects=True),
        cost_estimate=pl.CostEstimate(flops=0, bytes_accessed=250_000_000, transcendentals=0),
        name="gather_grads",
    )(own)
    return gathered.reshape(n * own.shape[0], own.shape[1])


def on_device(tokens, w_query, key_weight, value_weight, w_output, out_grad):
    sequence_length = tokens.shape[0]
    head_cols = w_query.shape[1]
    kv_cols = key_weight.shape[1]
    local_kv = kv_cols // HEAD_SIZE
    group_width = head_cols // kv_cols
    block_count = sequence_length // sequence_length
    score_scale = 1.0 / math.sqrt(HEAD_SIZE)
    tp_count = lax.axis_size("tp")
    blk_count = lax.axis_size("blk")
    weight_block = jnp.concatenate([w_query, key_weight, value_weight, w_output.T], axis=1)
    weight_rows, landed = gather_inputs(weight_block, tokens, out_grad, tp_count, blk_count)
    joint_cols = head_cols + 2 * kv_cols
    joint_rows = weight_rows[:, :joint_cols]
    output_cols = weight_rows[:, joint_cols:]
    inputs_by_cols = landed.reshape(2, blk_count * sequence_length, landed.shape[4])
    joint_full = jnp.dot(tokens, joint_rows, preferred_element_type=jnp.float32)
    query_full = joint_full[:, :head_cols]
    key_full = joint_full[:, head_cols : head_cols + kv_cols]
    value_full = joint_full[:, head_cols + kv_cols :]
    query_activation = query_full.astype(jnp.bfloat16)
    query_head_rows = query_activation.reshape(sequence_length, local_kv, group_width, HEAD_SIZE)
    key_activation = key_full.astype(jnp.bfloat16)
    key_head_rows = key_activation.reshape(sequence_length, local_kv, HEAD_SIZE)
    value_head_rows = value_full.astype(jnp.bfloat16).reshape(sequence_length, local_kv, HEAD_SIZE)
    block_ids = jnp.arange(block_count, dtype=jnp.int32)

    def forward_block(ignored, block_index):
        first_row = block_index * sequence_length
        soft_weights = causal_probs(query_head_rows, key_head_rows, first_row, score_scale).astype(
            jnp.bfloat16
        )
        head_block = jnp.einsum(
            "kgts,skd->tkgd", soft_weights, value_head_rows, preferred_element_type=jnp.float32
        )
        return (ignored, head_block.astype(jnp.bfloat16))

    ignored_carry, mix_blocks = lax.scan(forward_block, jnp.zeros((), jnp.int32), block_ids)
    head_mix = mix_blocks.reshape(sequence_length, head_cols)
    out_term = transposed_product(head_mix, output_cols)
    attn_out = lax.psum_scatter(out_term, "tp", scatter_dimension=1, tiled=True).astype(
        jnp.bfloat16
    )
    heads_gradient = (
        jnp.dot(out_grad, output_cols, preferred_element_type=jnp.float32)
        .astype(jnp.bfloat16)
        .reshape(sequence_length, local_kv, group_width, HEAD_SIZE)
    )

    def backward_block(kv_sums, block_index):
        first_row = block_index * sequence_length
        probs = causal_probs(query_head_rows, key_head_rows, first_row, score_scale)
        soft_weights = probs.astype(jnp.bfloat16)
        grad_probs = jnp.einsum(
            "tkgd,skd->kgts", heads_gradient, value_head_rows, preferred_element_type=jnp.float32
        )
        row_delta = jnp.sum(probs * grad_probs, axis=-1, keepdims=True)
        scores_gradient = (probs * (grad_probs - row_delta) * score_scale).astype(jnp.bfloat16)
        grad_query = jnp.einsum(
            "kgts,skd->tkgd", scores_gradient, key_head_rows, preferred_element_type=jnp.float32
        )
        key_total = kv_sums[0] + jnp.einsum(
            "uxyi,yuxz->iuz", scores_gradient, query_head_rows, preferred_element_type=jnp.float32
        )
        value_total = kv_sums[1] + jnp.einsum(
            "uxyi,yuxz->iuz", soft_weights, heads_gradient, preferred_element_type=jnp.float32
        )
        return ((key_total, value_total), grad_query.astype(jnp.bfloat16))

    empty_kv = jnp.zeros((sequence_length, local_kv, HEAD_SIZE), jnp.float32)
    kv_totals, query_blocks = lax.scan(backward_block, (empty_kv, empty_kv), block_ids)
    grad_query = query_blocks.reshape(sequence_length, head_cols)
    key_gradient = kv_totals[0].astype(jnp.bfloat16).reshape(sequence_length, kv_cols)
    value_gradient = kv_totals[1].astype(jnp.bfloat16).reshape(sequence_length, kv_cols)
    joined_grads = jnp.concatenate([grad_query, key_gradient, value_gradient], axis=1)
    input_term = transposed_product(joined_grads, joint_rows)
    tokens_grad = lax.psum_scatter(input_term, "tp", scatter_dimension=1, tiled=True).astype(
        jnp.bfloat16
    )
    grads_all = gather_grads(jnp.concatenate([joined_grads, head_mix], axis=1), blk_count)
    tokens_cols, out_grad_cols = inputs_by_cols[0], inputs_by_cols[1]
    joint_grad = leading_product(tokens_cols, grads_all[:, :joint_cols])
    query_grad = joint_grad[:, :head_cols]
    key_grad = joint_grad[:, head_cols : head_cols + kv_cols]
    value_grad = joint_grad[:, head_cols + kv_cols :]
    output_grad = leading_product(grads_all[:, joint_cols:], out_grad_cols)
    return (attn_out, tokens_grad, query_grad, key_grad, value_grad, output_grad)


def solution(mesh):
    placed = (
        P("blk", None),
        P("blk", "tp"),
        P("blk", "tp"),
        P("blk", "tp"),
        P("tp", "blk"),
        P("blk", None),
    )
    return jax.shard_map(
        on_device,
        mesh=mesh,
        in_specs=placed,
        out_specs=(
            P("blk", "tp"),
            P("blk", "tp"),
            P("blk", "tp"),
            P("blk", "tp"),
            P("blk", "tp"),
            P("tp", "blk"),
        ),
        check_vma=False,
    )
```

```python
import functools
import math

import jax
import jax.numpy as jnp
from jax import lax
from jax.experimental import pallas as pl
from jax.experimental.pallas import tpu as pltpu
from jax.sharding import PartitionSpec as P

HEAD_SIZE = 128


def transposed_product(first_operand, second_operand):
    return lax.dot_general(
        first_operand, second_operand, (((1,), (1,)), ((), ())), preferred_element_type=jnp.float32
    )


def leading_product(first_operand, second_operand):
    return lax.dot_general(
        first_operand, second_operand, (((0,), (0,)), ((), ())), preferred_element_type=jnp.float32
    )


def causal_probs(query_block, key_head_rows, first_row, score_scale):
    scores = (
        jnp.einsum("tkgd,skd->kgts", query_block, key_head_rows, preferred_element_type=jnp.float32)
        * score_scale
    )
    row_index = first_row + lax.broadcasted_iota(jnp.int32, scores.shape, 2)
    col_index = lax.broadcasted_iota(jnp.int32, scores.shape, 3)
    scores = jnp.where(col_index <= row_index, scores, -jnp.inf)
    row_max = jnp.max(scores, axis=-1, keepdims=True)
    powered = jnp.exp(scores - row_max)
    return powered / jnp.sum(powered, axis=-1, keepdims=True)


def remote(src, dst, send, recv, dest, axis="blk"):
    return pltpu.make_async_remote_copy(
        src_ref=src,
        dst_ref=dst,
        send_sem=send,
        recv_sem=recv,
        device_id={axis: dest},
        device_id_type=pl.DeviceIdType.MESH,
    )


def greet(n, parts=1):
    me = lax.axis_index("blk")
    barrier = pltpu.get_barrier_semaphore()
    for offset in range(1, n):
        pl.semaphore_signal(
            barrier,
            inc=1,
            device_id={"blk": lax.rem(me + offset, n)},
            device_id_type=pl.DeviceIdType.MESH,
        )
    mate = lax.axis_index("tp")
    for offset in range(1, parts):
        pl.semaphore_signal(
            barrier,
            inc=1,
            device_id={"tp": lax.rem(mate + offset, parts)},
            device_id_type=pl.DeviceIdType.MESH,
        )
    pl.semaphore_wait(barrier, n - 1 + parts - 1)


def chain_gather(n, own, out, chain_send, chain_recv, side_send, side_recv, own_sem, begin=None, between=None):
    me = lax.axis_index("blk")
    length = n // 2
    place, side = me // 2, lax.rem(me, 2)
    other = place * 2 + (1 - side)

    def along(way, origin, first):
        src = own if first else out.at[origin * 2 + side]
        step = 2 if way == 0 else -2
        return remote(
            src, out.at[origin * 2 + side], chain_send.at[way, origin], chain_recv.at[origin], me + step
        )

    def across(origin, first):
        src = own if first else out.at[origin * 2 + side]
        return remote(
            src, out.at[origin * 2 + side], side_send.at[origin], side_recv.at[origin], other
        )

    can = (place + 1 < length, place >= 1)
    for way in range(2):
        @pl.when(can[way])
        def _():
            along(way, place, True).start()

    across(place, True).start()
    if begin is not None:
        begin()
    mine = pltpu.make_async_copy(own, out.at[me], own_sem)
    mine.start()
    for step in range(1, length):
        for way in range(2):
            origin = place - step if way == 0 else place + step
            there = origin >= 0 if way == 0 else origin < length

            @pl.when(there)
            def _():
                along(way, origin, False).wait_recv()

            @pl.when(jnp.logical_and(there, can[way]))
            def _():
                along(way, origin, False).start()

            @pl.when(there)
            def _():
                across(origin, False).start()

        if between is not None:
            between(step)

    def finish():
        mine.wait()
        for step in range(length):
            for way in range(2):
                if step == 0 and way == 1:
                    continue
                origin = place - step if way == 0 else place + step
                there = origin >= 0 if way == 0 else origin < length

                @pl.when(there)
                def _():
                    across(origin, step == 0).wait_send()

            for way in range(2):
                origin = place - step if way == 0 else place + step
                there = origin >= 0 if way == 0 else origin < length

                @pl.when(jnp.logical_and(there, can[way]))
                def _():
                    along(way, origin, step == 0).wait_send()

        for origin in range(length):
            landed = out.at[origin * 2 + (1 - side)]
            remote(landed, landed, side_send.at[origin], side_recv.at[origin], other).wait_recv()

    return finish


def gather_semaphores(n):
    length = n // 2
    return [
        pltpu.SemaphoreType.DMA((2, length)),
        pltpu.SemaphoreType.DMA((length,)),
        pltpu.SemaphoreType.DMA((length,)),
        pltpu.SemaphoreType.DMA((length,)),
        pltpu.SemaphoreType.DMA,
    ]


def first_kernel(n, parts, weights, tokens, out_grad, out, landed_tokens, landed_grad, *sems):
    landed = (landed_tokens, landed_grad)
    gather_sems, (part_send, part_recv, part_own, mate_send, mate_recv) = sems[:5], sems[5:]
    me = lax.axis_index("blk")
    mate = lax.axis_index("tp")
    rows = tokens.shape[0] // parts
    cols = tokens.shape[1] // n
    first = pl.multiple_of(mate * rows, rows)
    greet(n, parts)

    def part(which, dest):
        at = pl.multiple_of(dest * cols, cols)
        return (tokens, out_grad)[which].at[pl.ds(first, rows), pl.ds(at, cols)]

    def sending(which, offset):
        dest = lax.rem(me + offset, n)
        return remote(
            part(which, dest),
            landed[which].at[me, mate],
            part_send.at[which, offset],
            part_recv.at[which, offset],
            dest,
        )

    def arriving(which, offset):
        origin = lax.rem(me + n - offset, n)
        here = landed[which].at[origin, mate]
        return remote(here, here, part_send.at[which, offset], part_recv.at[which, offset], origin)

    def sharing(which, offset, other):
        here = landed[which].at[lax.rem(me + n - offset, n), mate]
        dest = lax.rem(mate + other, parts)
        return remote(here, here, mate_send.at[which, offset, other], mate_recv.at[which, offset, other], dest, "tp")

    def shared(which, offset, other):
        source = lax.rem(mate + parts - other, parts)
        here = landed[which].at[lax.rem(me + n - offset, n), source]
        return remote(here, here, mate_send.at[which, offset, other], mate_recv.at[which, offset, other], source, "tp")

    own_parts = [
        pltpu.make_async_copy(part(which, me), landed[which].at[me, mate], part_own.at[which])
        for which in range(2)
    ]
    steps = n // 2 - 1

    def begin():
        for copy in own_parts:
            copy.start()
        for offset in range(1, n):
            for which in range(2):
                sending(which, offset).start()
        for copy in own_parts:
            copy.wait()
        for other in range(1, parts):
            for which in range(2):
                sharing(which, 0, other).start()

    def pass_on(offsets):
        for offset in offsets:
            for which in range(2):
                arriving(which, offset).wait_recv()
                for other in range(1, parts):
                    sharing(which, offset, other).start()

    def between(step):
        pass_on(range(1 + (step - 1) * (n - 1) // steps, 1 + step * (n - 1) // steps))

    finish = chain_gather(n, weights, out, *gather_sems, begin=begin, between=between)
    if steps == 0:
        pass_on(range(1, n))
    finish()
    for offset in range(1, n):
        for which in range(2):
            sending(which, offset).wait_send()
    for offset in range(n):
        for other in range(1, parts):
            for which in range(2):
                sharing(which, offset, other).wait_send()
                shared(which, offset, other).wait_recv()


def second_kernel(n, own, out, *sems):
    greet(n)
    chain_gather(n, own, out, *sems)()


def gather_inputs(weights, tokens, out_grad, tp_count, n):
    rows = tokens.shape[0] // tp_count
    cols = tokens.shape[1] // n
    anywhere = pl.BlockSpec(memory_space=pl.ANY)
    gathered, *landed = pl.pallas_call(
        functools.partial(first_kernel, n, tp_count),
        out_shape=(
            jax.ShapeDtypeStruct((n,) + weights.shape, weights.dtype),
            jax.ShapeDtypeStruct((n, tp_count, rows, cols), tokens.dtype),
            jax.ShapeDtypeStruct((n, tp_count, rows, cols), tokens.dtype),
        ),
        in_specs=[anywhere] * 3,
        out_specs=(anywhere,) * 3,
        scratch_shapes=gather_semaphores(n)
        + [
            pltpu.SemaphoreType.DMA((2, n)),
            pltpu.SemaphoreType.DMA((2, n)),
            pltpu.SemaphoreType.DMA((2,)),
            pltpu.SemaphoreType.DMA((2, n, tp_count)),
            pltpu.SemaphoreType.DMA((2, n, tp_count)),
        ],
        compiler_params=pltpu.CompilerParams(collective_id=0, has_side_effects=True),
        cost_estimate=pl.CostEstimate(flops=0, bytes_accessed=300_000_000, transcendentals=0),
        name="gather_inputs",
    )(weights, tokens, out_grad)
    return gathered.reshape(n * weights.shape[0], weights.shape[1]), landed


def gather_grads(own, n):
    anywhere = pl.BlockSpec(memory_space=pl.ANY)
    gathered = pl.pallas_call(
        functools.partial(second_kernel, n),
        out_shape=jax.ShapeDtypeStruct((n,) + own.shape, own.dtype),
        in_specs=[anywhere],
        out_specs=anywhere,
        scratch_shapes=gather_semaphores(n),
        compiler_params=pltpu.CompilerParams(collective_id=1, has_side_effects=True),
        cost_estimate=pl.CostEstimate(flops=0, bytes_accessed=250_000_000, transcendentals=0),
        name="gather_grads",
    )(own)
    return gathered.reshape(n * own.shape[0], own.shape[1])


def on_device(tokens, w_query, key_weight, value_weight, w_output, out_grad):
    sequence_length = tokens.shape[0]
    head_cols = w_query.shape[1]
    kv_cols = key_weight.shape[1]
    local_kv = kv_cols // HEAD_SIZE
    group_width = head_cols // kv_cols
    block_count = sequence_length // sequence_length
    score_scale = 1.0 / math.sqrt(HEAD_SIZE)
    tp_count = lax.axis_size("tp")
    blk_count = lax.axis_size("blk")
    weight_block = jnp.concatenate([w_query, key_weight, value_weight, w_output.T], axis=1)
    weight_rows, landed = gather_inputs(weight_block, tokens, out_grad, tp_count, blk_count)
    joint_cols = head_cols + 2 * kv_cols
    joint_rows = weight_rows[:, :joint_cols]
    output_cols = weight_rows[:, joint_cols:]
    tokens_cols, out_grad_cols = [
        one.reshape(blk_count * sequence_length, one.shape[3]) for one in landed
    ]
    joint_full = jnp.dot(tokens, joint_rows, preferred_element_type=jnp.float32)
    query_full = joint_full[:, :head_cols]
    key_full = joint_full[:, head_cols : head_cols + kv_cols]
    value_full = joint_full[:, head_cols + kv_cols :]
    query_activation = query_full.astype(jnp.bfloat16)
    query_head_rows = query_activation.reshape(sequence_length, local_kv, group_width, HEAD_SIZE)
    key_activation = key_full.astype(jnp.bfloat16)
    key_head_rows = key_activation.reshape(sequence_length, local_kv, HEAD_SIZE)
    value_head_rows = value_full.astype(jnp.bfloat16).reshape(sequence_length, local_kv, HEAD_SIZE)
    block_ids = jnp.arange(block_count, dtype=jnp.int32)

    def forward_block(ignored, block_index):
        first_row = block_index * sequence_length
        soft_weights = causal_probs(query_head_rows, key_head_rows, first_row, score_scale).astype(
            jnp.bfloat16
        )
        head_block = jnp.einsum(
            "kgts,skd->tkgd", soft_weights, value_head_rows, preferred_element_type=jnp.float32
        )
        return (ignored, head_block.astype(jnp.bfloat16))

    ignored_carry, mix_blocks = lax.scan(forward_block, jnp.zeros((), jnp.int32), block_ids)
    head_mix = mix_blocks.reshape(sequence_length, head_cols)
    out_term = transposed_product(head_mix, output_cols)
    attn_out = lax.psum_scatter(out_term, "tp", scatter_dimension=1, tiled=True).astype(
        jnp.bfloat16
    )
    heads_gradient = (
        jnp.dot(out_grad, output_cols, preferred_element_type=jnp.float32)
        .astype(jnp.bfloat16)
        .reshape(sequence_length, local_kv, group_width, HEAD_SIZE)
    )

    def backward_block(kv_sums, block_index):
        first_row = block_index * sequence_length
        probs = causal_probs(query_head_rows, key_head_rows, first_row, score_scale)
        soft_weights = probs.astype(jnp.bfloat16)
        grad_probs = jnp.einsum(
            "tkgd,skd->kgts", heads_gradient, value_head_rows, preferred_element_type=jnp.float32
        )
        row_delta = jnp.sum(probs * grad_probs, axis=-1, keepdims=True)
        scores_gradient = (probs * (grad_probs - row_delta) * score_scale).astype(jnp.bfloat16)
        grad_query = jnp.einsum(
            "kgts,skd->tkgd", scores_gradient, key_head_rows, preferred_element_type=jnp.float32
        )
        key_total = kv_sums[0] + jnp.einsum(
            "uxyi,yuxz->iuz", scores_gradient, query_head_rows, preferred_element_type=jnp.float32
        )
        value_total = kv_sums[1] + jnp.einsum(
            "uxyi,yuxz->iuz", soft_weights, heads_gradient, preferred_element_type=jnp.float32
        )
        return ((key_total, value_total), grad_query.astype(jnp.bfloat16))

    empty_kv = jnp.zeros((sequence_length, local_kv, HEAD_SIZE), jnp.float32)
    kv_totals, query_blocks = lax.scan(backward_block, (empty_kv, empty_kv), block_ids)
    grad_query = query_blocks.reshape(sequence_length, head_cols)
    key_gradient = kv_totals[0].astype(jnp.bfloat16).reshape(sequence_length, kv_cols)
    value_gradient = kv_totals[1].astype(jnp.bfloat16).reshape(sequence_length, kv_cols)
    joined_grads = jnp.concatenate([grad_query, key_gradient, value_gradient], axis=1)
    input_term = transposed_product(joined_grads, joint_rows)
    tokens_grad = lax.psum_scatter(input_term, "tp", scatter_dimension=1, tiled=True).astype(
        jnp.bfloat16
    )
    grads_all = gather_grads(jnp.concatenate([joined_grads, head_mix], axis=1), blk_count)
    joint_grad = leading_product(tokens_cols, grads_all[:, :joint_cols])
    query_grad = joint_grad[:, :head_cols]
    key_grad = joint_grad[:, head_cols : head_cols + kv_cols]
    value_grad = joint_grad[:, head_cols + kv_cols :]
    output_grad = leading_product(grads_all[:, joint_cols:], out_grad_cols)
    return (attn_out, tokens_grad, query_grad, key_grad, value_grad, output_grad)


def solution(mesh):
    placed = (
        P("blk", None),
        P("blk", "tp"),
        P("blk", "tp"),
        P("blk", "tp"),
        P("tp", "blk"),
        P("blk", None),
    )
    return jax.shard_map(
        on_device,
        mesh=mesh,
        in_specs=placed,
        out_specs=(
            P("blk", "tp"),
            P("blk", "tp"),
            P("blk", "tp"),
            P("blk", "tp"),
            P("blk", "tp"),
            P("tp", "blk"),
        ),
        check_vma=False,
    )
```
